32 devices in a mesh: groups: 2 (over y), ep: 4 (over z), tp: 4 (over x, core).
Axes of the slice: x: 2, y: 2, z: 4, core: 2. Of those that a mesh axis runs over, the one named last changes fastest.
Arguments:
- tokens: bfloat16 [384, 2048], P(('groups', 'ep'), 'tp'), parts along dimension 0, may hold values from -6 to 6
- norm_gain: float32 [2048], replicated, may hold values from 0.1 to 1.9
- route_ids: int32 [384, 8], P(('groups', 'ep')), parts along dimension 0, may hold values from 0 to 63, all different within a row; in each aligned block of 48 rows (0 to 47, 48 to 95, ...) at most 15 rows name the same one
- route_scores: float32 [384, 8], P(('groups', 'ep')), parts along dimension 0, may hold values from 0.05 to 1
- gate_weight: bfloat16 [128, 1024, 2048], P(('groups', 'ep'), 'tp'), parts along dimension 0, may hold values from -0.125 to 0.125
- up_weight: bfloat16 [128, 1024, 2048], P(('groups', 'ep'), 'tp'), parts along dimension 0, may hold values from -0.125 to 0.125
- down_weight: bfloat16 [128, 2048, 1024], P(('groups', 'ep'), None, 'tp'), parts along dimension 0, may hold values from -0.1875 to 0.1875
- delta_codes: bfloat16 [8, 4, 256, 128], P(('groups', 'ep'), 'tp'), parts along dimension 0, may hold values from -4 to 4
- delta_exps: int32 [8, 4, 256], P(('groups', 'ep'), 'tp'), parts along dimension 0, may hold values from -7 to -4
- delta_owner: int32 [8, 4, 256, 1], P(('groups', 'ep'), 'tp'), parts along dimension 0, may hold values from 0 to 3; in each aligned block of 256 rows (0 to 255, 256 to 511, ..., all dimensions but the last counted through in order) at most 160 rows name the same one
- delta_places: int32 [8, 4, 256], P(('groups', 'ep'), 'tp'), parts along dimension 0, may hold values from 0 to 49151
Outputs:
- mixed: bfloat16 [384, 2048], P(('groups', 'ep'), 'tp'), parts along dimension 0
The draws below stay inside these ranges and needn't reach their ends.
There are 2 independent parts, one for each index of `groups`. The reference program is written for one: setup_inputs(seed, part) draws one part's arguments, and reference() takes and returns one part's arrays. A program takes and returns all parts, laid end to end along the dimension named above; an argument that names none is the same for every part. Nothing has to cross between parts.
Inputs may be any that keep to these rules, and one draw needn't show every extreme that they name: `route_ids`: each row names 8 different experts. In the 48 rows of one device (aligned blocks of 48 rows) no expert is named by more than 15 rows. `delta_owner`: in the 256 blocks of one learner shard (aligned blocks of 256 rows) no owner is named more than 160 times.
All inputs are finite; a program needn't handle non-finite values.
Results may differ from the reference program's by a relative error of at most 0.012.
Values may be sent and summed in bfloat16 or wider, within the bound.
A program may use at most 320 MiB of HBM per device.

```python
import math
import jax
import jax.numpy as jnp
import numpy as np
from jax import lax

D = 2048
FF = 1024
EXPERTS = 64
TOP = 8
BLOCK = 128
ROWS = 48
NBLK = 256
TOKENS = 192
CAP = 15
EXP_DEV = 16
BCAP = 160
FF_TP = 256
FF_ROWS = 64
D_ROWS = 512
PLACES = 3072
N_EP = 4
N_TP = 4


def place_ends(drawn, key, low, high):
    extent = drawn.shape
    place = [jax.random.randint(jax.random.fold_in(key, axis), (), 0, extent[axis]) for axis in range(len(extent))]
    drawn = drawn.at[tuple(place)].set(low)
    longest = extent.index(max(extent))
    place[longest] = (place[longest] + 1) % extent[longest]
    return drawn.at[tuple(place)].set(high)


def levels(own_key, dims, pieces, low, high):
    factor_of, own = 1.0, jax.random.fold_in(own_key, 6)
    for axis_at, parts in pieces:
        draws = jnp.exp(jax.random.uniform(jax.random.fold_in(own, axis_at), (parts,), jnp.float32, low / len(pieces), high / len(pieces)))
        factor_of = factor_of * jnp.repeat(draws, dims[axis_at] // parts).reshape([-1 if axis == axis_at else 1 for axis in range(len(dims))])
    return factor_of


def deal_out(stream_key, own, number, rows, amount, top, most, lean):
    sequence = jax.random.permutation(stream_key, amount)
    packed, ordinary = portions_of(amount, rows * top, most, lean, True), portions_of(amount, rows * top, most, lean, False)
    places = jnp.arange(amount)

    def named(tallies, offset_by):
        used = int((tallies > 0).sum())
        fixed = max(1, used // 4)
        shifted = fixed + (places - fixed + offset_by * (used - fixed)) % max(1, amount - fixed)
        return jnp.zeros((amount,), jnp.int32).at[sequence[jnp.where(places < fixed, places, shifted)]].set(jnp.asarray(tallies, jnp.int32))

    tallies = jnp.where(number % 4 == 0, named(packed, number // 4), named(ordinary, number - number // 4 - 1))
    mixed = jax.random.permutation(jax.random.fold_in(own, 3), amount)
    donor, taker = mixed[0:amount // 2 * 2:2], mixed[1:amount // 2 * 2:2]
    room = jnp.minimum(tallies[donor] - 1, most - tallies[taker]) // 2
    room = jnp.where((donor == sequence[0]) | (taker == sequence[0]) | (tallies[taker] == 0), 0, jnp.maximum(room, 0))
    shifted = jax.random.randint(jax.random.fold_in(own, 4), (amount // 2,), 0, 1 << 20) % (room + 1)
    tallies = tallies.at[donor].add(-shifted).at[taker].add(shifted)
    members = jnp.searchsorted(jnp.cumsum(tallies), jnp.arange(rows * top), side="right").astype(jnp.int32)
    listing = members.reshape(top, rows).T
    listing = listing[jax.random.permutation(jax.random.fold_in(own, 1), rows)]
    offset_by = jax.random.randint(jax.random.fold_in(own, 2), (rows, 1), 0, top)
    return jnp.take_along_axis(listing, (jnp.arange(top)[None, :] + offset_by) % top, axis=1)


def portions_of(amount, total, reach, skew, full):
    loads = [(1 << 20) // math.isqrt(standing ** skew) + 1 for standing in range(1, amount + 1)]
    largest = reach if full else min(reach, max(-(-total // amount), total * loads[0] // sum(loads)))
    least = 1 if total - largest >= amount - 1 else 0
    holding, surplus = [largest] + [least] * (amount - 1), total - largest - least * (amount - 1)
    while surplus > 0:
        movable = [i for i in range(1, amount) if holding[i] < largest] or [i for i in range(1, amount) if holding[i] < reach]
        mass, left = sum([loads[i] for i in movable]), surplus
        for i in movable:
            addition = min(reach - holding[i], max(1, left * loads[i] // mass), surplus)
            holding[i] = holding[i] + addition
            surplus = surplus - addition
    return np.array(holding)


def gaussian(stream_key, dims, scale, bound, shards=(), kind=jnp.bfloat16):
    array = jax.random.normal(stream_key, dims, jnp.float32) * scale
    if len(shards) > 0:
        array = levels(stream_key, dims, shards, -0.22, 0.18) * array
    return jnp.clip(array, min=-bound, max=bound).astype(kind)


def setup_inputs(seed: int = 0, part: int = 0) -> dict:
    seeds = jax.random.split(jax.random.key(seed), 12)
    part_keys = jax.random.split(jax.random.fold_in(seeds[11], part), 12)
    tokens = gaussian(part_keys[0], (TOKENS, D), 1.0, 6.0, ((0, 4), (1, 4)))
    norm_gain = jnp.clip(1.0 + 0.18 * jax.random.normal(seeds[1], (D,), jnp.float32), 0.1, 1.9)
    route_ids_keys = jax.random.split(jax.random.fold_in(part_keys[2], 1), TOKENS // ROWS)
    route_ids_turns = jax.random.permutation(jax.random.fold_in(part_keys[2], 3), TOKENS // ROWS)
    route_ids = jax.vmap(lambda own, number: deal_out(jax.random.fold_in(part_keys[2], 2), own, number, ROWS, EXPERTS, TOP, CAP, 2))(route_ids_keys, route_ids_turns).reshape((TOKENS, TOP))
    route_scores = jnp.clip(jnp.exp(math.log(1.0) - 2.9957323 * jax.random.uniform(part_keys[3], (TOKENS, TOP), jnp.float32) ** levels(part_keys[3], (TOKENS, TOP), ((0, 4),), -0.2, 0.2)), 0.05, 1.0)
    gate_weight = gaussian(part_keys[4], (EXPERTS, FF, D), D ** -0.5, 0.125, ((0, 4), (1, 4)))
    up_weight = gaussian(part_keys[5], (EXPERTS, FF, D), D ** -0.5, 0.125, ((0, 4), (1, 4)))
    down_weight = gaussian(part_keys[6], (EXPERTS, D, FF), FF ** -0.5, 0.1875, ((0, 4), (2, 4)))
    delta_codes = gaussian(part_keys[7], (N_EP, N_TP, NBLK, BLOCK), 1.0, 4.0, ((0, 4), (1, 4)))
    delta_exps = place_ends(jax.random.randint(part_keys[8], (N_EP, N_TP, NBLK), -7, -3), jax.random.fold_in(part_keys[8], 1), -7, (-3) - 1).astype(jnp.int32)
    delta_owner_keys = jax.random.split(jax.random.fold_in(part_keys[9], 1), N_EP * N_TP * NBLK // NBLK)
    delta_owner_turns = jax.random.permutation(jax.random.fold_in(part_keys[9], 3), N_EP * N_TP * NBLK // NBLK)
    delta_owner = jax.vmap(lambda own, number: deal_out(jax.random.fold_in(part_keys[9], 2), own, number, NBLK, N_EP, 1, BCAP, 2))(delta_owner_keys, delta_owner_turns).reshape((N_EP, N_TP, NBLK, 1))
    delta_places = place_ends(jax.random.randint(part_keys[10], (N_EP, N_TP, NBLK), 0, EXP_DEV * PLACES), jax.random.fold_in(part_keys[10], 1), 0, (EXP_DEV * PLACES) - 1).astype(jnp.int32)
    return dict(tokens=tokens, norm_gain=norm_gain, route_ids=route_ids, route_scores=route_scores, gate_weight=gate_weight, up_weight=up_weight, down_weight=down_weight, delta_codes=delta_codes, delta_exps=delta_exps, delta_owner=delta_owner, delta_places=delta_places)


EPS = 1e-06

def block_targets(delta_owner, delta_places):
    learner = jnp.arange(N_EP, dtype=jnp.int32)[:, None, None]
    column = jnp.arange(N_TP, dtype=jnp.int32)[None, :, None]
    expert = delta_owner[..., 0] * EXP_DEV + delta_places // PLACES
    spot = delta_places % PLACES
    per_row = D // BLOCK
    per_down = FF_TP // BLOCK
    span = FF_ROWS * per_row
    is_down = spot >= 2 * span
    matrix_pick = jnp.minimum(spot // span, 1)
    remain = spot % span
    ff_row = column * FF_TP + learner * FF_ROWS + remain // per_row
    gate_flat = (expert * FF + ff_row) * per_row + remain % per_row
    down_spot = jnp.maximum(spot - 2 * span, 0)
    d_row = learner * D_ROWS + down_spot // per_down
    down_flat = (expert * D + d_row) * (FF // BLOCK) + column * per_down + down_spot % per_down
    return (is_down, matrix_pick, gate_flat.astype(jnp.int32), down_flat.astype(jnp.int32))

def apply_blocks(weight, flat, chosen, delta_values):
    count = weight.size // BLOCK
    target = jnp.where(chosen, flat, count).reshape(-1).astype(jnp.int32)
    table = weight.astype(jnp.float32).reshape(count, BLOCK)
    table = table.at[target].add(delta_values.reshape(-1, BLOCK), mode='drop')
    return table.reshape(weight.shape).astype(jnp.bfloat16)

def reference(tokens, norm_gain, route_ids, route_scores, gate_weight, up_weight, down_weight, delta_codes, delta_exps, delta_owner, delta_places):
    delta_values = delta_codes.astype(jnp.float32) * jnp.exp2(delta_exps.astype(jnp.float32))[..., None]
    is_down, matrix_pick, gate_flat, down_flat = block_targets(delta_owner, delta_places)
    new_gate = apply_blocks(gate_weight, gate_flat, jnp.logical_and(jnp.logical_not(is_down), matrix_pick == 0), delta_values)
    new_up = apply_blocks(up_weight, gate_flat, jnp.logical_and(jnp.logical_not(is_down), matrix_pick == 1), delta_values)
    new_down = apply_blocks(down_weight, down_flat, is_down, delta_values)
    floats = tokens.astype(jnp.float32)
    scaling = lax.rsqrt(lax.optimization_barrier(jnp.mean(floats * floats, axis=1, keepdims=True)) + EPS)
    normed = (floats * scaling * norm_gain[None, :]).astype(jnp.bfloat16)
    shares = route_scores / lax.optimization_barrier(jnp.sum(route_scores, axis=1, keepdims=True))
    held = N_EP * CAP

    def one_expert(expert, mixed):
        hits = route_ids == expert
        weight_share = lax.optimization_barrier(jnp.sum(jnp.where(hits, shares, 0.0), axis=1))
        picked = jnp.any(hits, axis=1)
        order = jnp.argsort(jnp.where(picked, 0, 1).astype(jnp.int32), stable=True)[:held].astype(jnp.int32)
        chosen_rows = normed[order]
        gate = jnp.dot(chosen_rows, new_gate[expert].T, preferred_element_type=jnp.float32)
        up = jnp.dot(chosen_rows, new_up[expert].T, preferred_element_type=jnp.float32)
        hidden = (jax.nn.silu(gate) * up).astype(jnp.bfloat16)
        down_rows = new_down[expert]
        summed = jnp.zeros((held, D), jnp.float32)
        for column in range(N_TP):
            part = jnp.dot(hidden[:, column * FF_TP:(column + 1) * FF_TP], down_rows[:, column * FF_TP:(column + 1) * FF_TP].T, preferred_element_type=jnp.float32)
            summed = summed + lax.optimization_barrier(part.astype(jnp.bfloat16)).astype(jnp.float32)
        return mixed.at[order].add(weight_share[order][:, None] * summed)
    mixed = lax.fori_loop(0, EXPERTS, one_expert, jnp.zeros((TOKENS, D), jnp.float32))
    return mixed.astype(jnp.bfloat16)
```

```python
import functools

import jax
import jax.numpy as jnp
from jax import lax
from jax.experimental import pallas as pl
from jax.experimental.pallas import tpu as pltpu
from jax.sharding import PartitionSpec as P

EXPERTS = 64
TOP = 8
CAP = 15


EPS = 1e-06


def row_norm(values, gain, width):
    floats = values.astype(jnp.float32)
    scaling = lax.rsqrt(jnp.sum(floats * floats, axis=-1, keepdims=True) / width + EPS)
    return (floats * scaling * gain).astype(jnp.bfloat16)


def routed(
    tokens,
    norm_gain,
    route_ids,
    route_scores,
    gate_weight,
    up_weight,
    down_weight,
    delta_codes,
    delta_exps,
    delta_owner,
    delta_places,
):
    ep_count = lax.axis_size("ep")
    ep_rank = lax.axis_index("ep")
    exp_dev, ff_local, width = gate_weight.shape
    block = delta_codes.shape[3]
    block_count = delta_codes.shape[2]
    per_row = width // block
    per_down = ff_local // block
    ff_rows = ff_local // ep_count
    d_rows = width // ep_count
    span = ff_rows * per_row
    places = 2 * span + d_rows * per_down
    bucket = block_count * 5 // (2 * ep_count)
    gate_blocks = exp_dev * ff_local * per_row
    table_rows = 3 * gate_blocks
    delta_values = (
        delta_codes[0, 0].astype(jnp.float32)
        * jnp.exp2(delta_exps[0, 0].astype(jnp.float32))[:, None]
    ).astype(jnp.bfloat16)
    placing = delta_places[0, 0]
    local_expert = placing // places
    spot = placing % places
    remain = spot % span
    matrix_pick = jnp.minimum(spot // span, 1)
    gate_slot = (
        matrix_pick * gate_blocks
        + (local_expert * ff_local + ep_rank * ff_rows + remain // per_row) * per_row
        + remain % per_row
    )
    down_spot = jnp.maximum(spot - 2 * span, 0)
    down_slot = (
        2 * gate_blocks
        + (local_expert * width + ep_rank * d_rows + down_spot // per_down) * per_down
        + down_spot % per_down
    )
    target = jnp.where(spot < 2 * span, gate_slot, down_slot)
    owners = delta_owner[0, 0, :, 0]
    owner_hits = (owners[:, None] == jnp.arange(ep_count, dtype=jnp.int32)[None, :]).astype(
        jnp.int32
    )
    owner_before = jnp.cumsum(owner_hits, axis=0) - owner_hits
    position = owners * bucket + jnp.sum(owner_before * owner_hits, axis=1)
    send_match = position[None, :] == jnp.arange(ep_count * bucket, dtype=jnp.int32)[:, None]
    send_values = jnp.dot(
        send_match.astype(jnp.bfloat16), delta_values, preferred_element_type=jnp.float32
    ).astype(jnp.bfloat16)
    target_code = jnp.dot(
        send_match.astype(jnp.float32),
        (target + 1).astype(jnp.float32),
        precision=lax.Precision.HIGHEST,
    ).astype(jnp.int32)
    send_target = jnp.where(target_code > 0, target_code - 1, table_rows)
    got_values, got_target = (
        lax.all_to_all(
            send_values.reshape(ep_count, bucket, block),
            "ep",
            split_axis=0,
            concat_axis=0,
            tiled=True,
        ),
        lax.all_to_all(
            send_target.reshape(ep_count, bucket), "ep", split_axis=0, concat_axis=0, tiled=True
        ),
    )
    got_flat = got_target.reshape(-1)
    got_rows = got_values.reshape(-1, block)
    same_target = (got_flat[:, None] == got_flat[None, :]).astype(jnp.bfloat16)
    combined = jnp.dot(same_target, got_rows, preferred_element_type=jnp.float32)

    def updated(weight, base):
        flat_weight = weight.reshape(-1, block)
        offset_ids = got_flat - base
        usable = jnp.logical_and(offset_ids >= 0, offset_ids < gate_blocks)
        row_index = jnp.where(usable, offset_ids, gate_blocks).astype(jnp.int32)
        fetched = jnp.take(flat_weight, jnp.minimum(row_index, gate_blocks - 1), axis=0).astype(
            jnp.float32
        )
        new_rows = (fetched + combined).astype(jnp.bfloat16)
        return flat_weight.at[row_index].set(new_rows, mode="drop").reshape(weight.shape)

    new_gate = updated(gate_weight, 0)
    new_up = updated(up_weight, gate_blocks)
    new_down = updated(down_weight, 2 * gate_blocks)
    token_rows, slice_width = tokens.shape
    picks = route_ids.reshape(-1)
    expert_hits = (picks[:, None] == jnp.arange(EXPERTS, dtype=jnp.int32)[None, :]).astype(
        jnp.int32
    )
    expert_before = jnp.cumsum(expert_hits, axis=0) - expert_hits
    slot = picks * CAP + jnp.sum(expert_before * expert_hits, axis=1)
    slot_match = (slot[None, :] == jnp.arange(EXPERTS * CAP, dtype=jnp.int32)[:, None]).reshape(
        EXPERTS * CAP, token_rows, TOP
    )
    full_rows = lax.all_gather(tokens, "tp", axis=1, tiled=True)
    outgoing = row_norm(full_rows, norm_gain, width)
    feature_count = outgoing.shape[1]
    slot_rows = jnp.any(slot_match, axis=2).astype(jnp.bfloat16)
    sending = jnp.dot(slot_rows, outgoing, preferred_element_type=jnp.float32).astype(jnp.bfloat16)
    sending = sending.reshape(ep_count, exp_dev, CAP, feature_count)
    normed = lax.all_to_all(sending, "ep", split_axis=0, concat_axis=0, tiled=True)
    gate = jnp.einsum("secd,efd->secf", normed, new_gate, preferred_element_type=jnp.float32)
    up = jnp.einsum("secd,efd->secf", normed, new_up, preferred_element_type=jnp.float32)
    gate, up = (gate, up)
    hidden = (jax.nn.silu(gate) * up).astype(jnp.bfloat16)
    partial_value = jnp.einsum(
        "secf,edf->secd", hidden, new_down, preferred_element_type=jnp.float32
    ).astype(jnp.bfloat16)
    results = lax.all_to_all(partial_value, "ep", split_axis=0, concat_axis=0, tiled=True)
    result_width = results.shape[3]
    flat_results = results.reshape(EXPERTS * CAP, result_width).astype(jnp.float32)
    shares = route_scores / jnp.sum(route_scores, axis=1, keepdims=True)
    slot_shares = jnp.sum(jnp.where(slot_match, shares[None, :, :], 0.0), axis=2)
    weighted = jnp.einsum("st,sd->td", slot_shares, flat_results, precision=lax.Precision.HIGHEST)
    return lax.psum_scatter(weighted.astype(jnp.bfloat16), "tp", scatter_dimension=1, tiled=True)


MAX_ROWS = 512
SUB = 1 << 15
META_ROWS = 32


def split_parts(whole):
    high = whole.astype(jnp.bfloat16)
    rest = whole - high.astype(jnp.float32)
    middle = rest.astype(jnp.bfloat16)
    low = (rest - middle.astype(jnp.float32)).astype(jnp.bfloat16)
    return [high, middle, low]


def expert_kernel(
    table, begins, rank, tokens, gain, ids, shares, values, gate, up, down, out, normed, total
):
    step = pl.program_id(0)
    exp_dev = pl.num_programs(0)
    ep_count, tp_count, rows, part = tokens.shape
    width = tp_count * part

    @pl.when(step == 0)
    def _():
        for i in range(ep_count):
            scale = jnp.zeros((rows, 1), jnp.float32)
            for c in range(tp_count):
                floats = tokens[i, c].astype(jnp.float32)
                scale += jnp.sum(floats * floats, axis=1, keepdims=True)
            scale = lax.rsqrt(scale / width + EPS)
            for c in range(tp_count):
                span = slice(c * part, (c + 1) * part)
                normed[i * rows : (i + 1) * rows, span] = (
                    tokens[i, c].astype(jnp.float32) * scale * gain[:, span]
                ).astype(jnp.bfloat16)

    line = lax.broadcasted_iota(jnp.int32, (16, 128), 0)
    for m, weight in enumerate((gate, up, down)):

        @pl.loop(begins[3 * step + m], begins[3 * step + m + 1])
        def _(b):
            place = table[b]
            row, column = place // 16, place % 16
            first = pl.multiple_of(row // 16 * 16, 16)
            where = (0, pl.ds(first, 16), pl.ds(pl.multiple_of(column * 128, 128), 128))
            added = jnp.where(line == row - first, values[pl.ds(b, 1), :], 0.0)
            weight[where] = (weight[where].astype(jnp.float32) + added).astype(jnp.bfloat16)

    dims = (((1,), (1,)), ((), ()))
    share = jnp.sum(
        jnp.where(ids[...] == rank[0] * exp_dev + step, shares[...], 0.0), axis=1, keepdims=True
    )
    gated = lax.dot_general(normed[...], gate[0], dims, preferred_element_type=jnp.float32)
    upped = lax.dot_general(normed[...], up[0], dims, preferred_element_type=jnp.float32)
    hidden = (gated / (1.0 + jnp.exp(-gated)) * upped * share).astype(jnp.bfloat16)

    for c in range(tp_count):
        span = slice(c * part, (c + 1) * part)
        term = lax.dot_general(hidden, down[0, span, :], dims, preferred_element_type=jnp.float32)

        @pl.when(step == 0)
        def _():
            total[:, span] = term

        @pl.when(step > 0)
        def _():
            total[:, span] += term

    @pl.when(step == exp_dev - 1)
    def _():
        for i in range(ep_count):
            for c in range(tp_count):
                out[i, c] = total[
                    i * rows : (i + 1) * rows, c * part : (c + 1) * part
                ].astype(jnp.bfloat16)


def expert_sums(table, begins, rank, tokens, gain, ids, shares, values, gate, up, down):
    ep_count, tp_count, rows, part = tokens.shape
    exp_dev, ff_local, width = gate.shape

    def held(array):
        return pl.BlockSpec(array.shape, lambda step, *_: (0,) * array.ndim)

    def one(array):
        return pl.BlockSpec((1,) + array.shape[1:], lambda step, *_: (step, 0, 0))

    return pl.pallas_call(
        expert_kernel,
        out_shape=jax.ShapeDtypeStruct(tokens.shape, jnp.bfloat16),
        grid_spec=pltpu.PrefetchScalarGridSpec(
            num_scalar_prefetch=3,
            grid=(exp_dev,),
            in_specs=[held(tokens), held(gain), held(ids), held(shares), held(values)]
            + [one(gate), one(up), one(down)],
            out_specs=held(tokens),
            scratch_shapes=[
                pltpu.VMEM((ep_count * rows, width), jnp.bfloat16),
                pltpu.VMEM((ep_count * rows, width), jnp.float32),
            ],
        ),
        compiler_params=pltpu.CompilerParams(vmem_limit_bytes=40 << 20),
    )(table, begins, rank, tokens, gain, ids, shares, values, gate, up, down)


def sorted_updates(owned, placing, values, ep_count, exp_dev, ff_local, width, limit):
    block = values.shape[1]
    count = values.shape[0]
    learner = jnp.arange(count, dtype=jnp.int32) // (count // ep_count)
    per_row, per_down = width // block, ff_local // block
    ff_rows, d_rows = ff_local // ep_count, width // ep_count
    span = ff_rows * per_row
    places = 2 * span + d_rows * per_down
    spot = placing % places
    matrix = jnp.minimum(spot // span, 2)
    remain = spot - matrix * span
    row_up, column_up = learner * ff_rows + remain // per_row, remain % per_row
    row_down, column_down = learner * d_rows + remain // per_down, remain % per_down
    row = jnp.where(matrix == 2, row_down, row_up)
    column = jnp.where(matrix == 2, column_down, column_up)
    target = (placing // places * 3 + matrix) * SUB + row * 16 + column
    target = jnp.where(owned, target, 1 << 30)
    order = jnp.arange(count, dtype=jnp.int32)
    ahead = jnp.logical_or(
        target[None, :] < target[:, None],
        jnp.logical_and(target[None, :] == target[:, None], order[None, :] < order[:, None]),
    )
    position = jnp.sum(ahead.astype(jnp.int32), axis=1)
    chosen = position[None, :] == jnp.arange(limit, dtype=jnp.int32)[:, None]
    ordered = jnp.sum(jnp.where(chosen, target[None, :], 0), axis=1)
    same = (ordered[:, None] == target[None, :]).astype(jnp.bfloat16)
    combined = jnp.dot(same, values, preferred_element_type=jnp.float32)
    repeated = jnp.concatenate([jnp.zeros((1,), jnp.bool_), ordered[1:] == ordered[:-1]])
    combined = jnp.where(repeated[:, None], 0.0, combined)
    edges = jnp.arange(3 * exp_dev + 1, dtype=jnp.int32) * SUB
    begins = jnp.sum((target[None, :] < edges[:, None]).astype(jnp.int32), axis=1)
    return ordered % SUB, begins, combined


def gathered(
    tokens,
    norm_gain,
    route_ids,
    route_scores,
    gate_weight,
    up_weight,
    down_weight,
    delta_codes,
    delta_exps,
    delta_owner,
    delta_places,
):
    ep_count, tp_count = lax.axis_size("ep"), lax.axis_size("tp")
    ep_rank = lax.axis_index("ep")
    exp_dev, ff_local, width = gate_weight.shape
    block_count, block = delta_codes.shape[2:]
    rows = tokens.shape[0]
    limit = block_count * 5 // (2 * ep_count) * ep_count

    delta_values = (
        delta_codes[0, 0].astype(jnp.float32)
        * jnp.exp2(delta_exps[0, 0].astype(jnp.float32))[:, None]
    ).astype(jnp.bfloat16)
    placing = delta_places[0, 0]
    shares = route_scores / jnp.sum(route_scores, axis=1, keepdims=True)
    numbers = [delta_owner[0, 0, :, 0], placing // 256, placing % 256]
    meta = jnp.concatenate(
        [number.astype(jnp.bfloat16) for number in numbers]
        + [route_ids.reshape(-1).astype(jnp.bfloat16)]
        + split_parts(shares.reshape(-1))
    )
    meta = jnp.pad(meta, (0, META_ROWS * block - meta.shape[0])).reshape(META_ROWS, block)
    got = lax.all_gather(jnp.concatenate([delta_values, meta]), "ep")
    got_tokens = lax.all_gather(tokens, ("ep", "tp"))

    got_values = got[:, :block_count].reshape(-1, block)
    got_meta = got[:, block_count:].reshape(ep_count, -1)
    listed = got_meta[:, : 3 * block_count].reshape(ep_count, 3, block_count).astype(jnp.int32)
    owner, high, low = (listed[:, k].reshape(-1) for k in range(3))
    start, picks = 3 * block_count, rows * TOP
    pieces = got_meta[:, start : start + 4 * picks].reshape(ep_count, 4, picks).astype(jnp.float32)
    ids = pieces[:, 0].astype(jnp.int32).reshape(-1, TOP)
    all_shares = (pieces[:, 1] + pieces[:, 2] + pieces[:, 3]).reshape(-1, TOP)
    table, begins, values = sorted_updates(
        owner == ep_rank, high * 256 + low, got_values, ep_count, exp_dev, ff_local, width, limit
    )
    sums = expert_sums(
        table,
        begins,
        ep_rank.reshape(1).astype(jnp.int32),
        got_tokens.reshape((ep_count, tp_count) + tokens.shape),
        norm_gain.reshape(1, -1),
        ids,
        all_shares,
        values,
        gate_weight,
        up_weight,
        down_weight,
    )
    return lax.psum_scatter(
        sums.reshape((ep_count * tp_count,) + tokens.shape), ("ep", "tp"), scatter_dimension=0
    )


def per_device(*args):
    few = args[0].shape[0] * lax.axis_size("ep") <= MAX_ROWS
    return gathered(*args) if few else routed(*args)


def solution(mesh):
    placed = (
        P(("groups", "ep"), "tp"),
        P(),
        P(("groups", "ep"), None),
        P(("groups", "ep"), None),
        P(("groups", "ep"), "tp", None),
        P(("groups", "ep"), "tp", None),
        P(("groups", "ep"), None, "tp"),
        P(("groups", "ep"), "tp", None, None),
        P(("groups", "ep"), "tp", None),
        P(("groups", "ep"), "tp", None, None),
        P(("groups", "ep"), "tp", None),
    )
    return jax.shard_map(
        per_device, mesh=mesh, in_specs=placed, out_specs=P(("groups", "ep"), "tp"), check_vma=False
    )
```

```python
import functools

import jax
import jax.numpy as jnp
from jax import lax
from jax.experimental import pallas as pl
from jax.experimental.pallas import tpu as pltpu
from jax.sharding import PartitionSpec as P

EXPERTS = 64
TOP = 8
CAP = 15


EPS = 1e-06


def row_norm(values, gain, width):
    floats = values.astype(jnp.float32)
    scaling = lax.rsqrt(jnp.sum(floats * floats, axis=-1, keepdims=True) / width + EPS)
    return (floats * scaling * gain).astype(jnp.bfloat16)


def routed(
    tokens,
    norm_gain,
    route_ids,
    route_scores,
    gate_weight,
    up_weight,
    down_weight,
    delta_codes,
    delta_exps,
    delta_owner,
    delta_places,
):
    ep_count = lax.axis_size("ep")
    ep_rank = lax.axis_index("ep")
    exp_dev, ff_local, width = gate_weight.shape
    block = delta_codes.shape[3]
    block_count = delta_codes.shape[2]
    per_row = width // block
    per_down = ff_local // block
    ff_rows = ff_local // ep_count
    d_rows = width // ep_count
    span = ff_rows * per_row
    places = 2 * span + d_rows * per_down
    bucket = block_count * 5 // (2 * ep_count)
    gate_blocks = exp_dev * ff_local * per_row
    table_rows = 3 * gate_blocks
    delta_values = (
        delta_codes[0, 0].astype(jnp.float32)
        * jnp.exp2(delta_exps[0, 0].astype(jnp.float32))[:, None]
    ).astype(jnp.bfloat16)
    placing = delta_places[0, 0]
    local_expert = placing // places
    spot = placing % places
    remain = spot % span
    matrix_pick = jnp.minimum(spot // span, 1)
    gate_slot = (
        matrix_pick * gate_blocks
        + (local_expert * ff_local + ep_rank * ff_rows + remain // per_row) * per_row
        + remain % per_row
    )
    down_spot = jnp.maximum(spot - 2 * span, 0)
    down_slot = (
        2 * gate_blocks
        + (local_expert * width + ep_rank * d_rows + down_spot // per_down) * per_down
        + down_spot % per_down
    )
    target = jnp.where(spot < 2 * span, gate_slot, down_slot)
    owners = delta_owner[0, 0, :, 0]
    owner_hits = (owners[:, None] == jnp.arange(ep_count, dtype=jnp.int32)[None, :]).astype(
        jnp.int32
    )
    owner_before = jnp.cumsum(owner_hits, axis=0) - owner_hits
    position = owners * bucket + jnp.sum(owner_before * owner_hits, axis=1)
    send_match = position[None, :] == jnp.arange(ep_count * bucket, dtype=jnp.int32)[:, None]
    send_values = jnp.dot(
        send_match.astype(jnp.bfloat16), delta_values, preferred_element_type=jnp.float32
    ).astype(jnp.bfloat16)
    target_code = jnp.dot(
        send_match.astype(jnp.float32),
        (target + 1).astype(jnp.float32),
        precision=lax.Precision.HIGHEST,
    ).astype(jnp.int32)
    send_target = jnp.where(target_code > 0, target_code - 1, table_rows)
    got_values, got_target = (
        lax.all_to_all(
            send_values.reshape(ep_count, bucket, block),
            "ep",
            split_axis=0,
            concat_axis=0,
            tiled=True,
        ),
        lax.all_to_all(
            send_target.reshape(ep_count, bucket), "ep", split_axis=0, concat_axis=0, tiled=True
        ),
    )
    got_flat = got_target.reshape(-1)
    got_rows = got_values.reshape(-1, block)
    same_target = (got_flat[:, None] == got_flat[None, :]).astype(jnp.bfloat16)
    combined = jnp.dot(same_target, got_rows, preferred_element_type=jnp.float32)

    def updated(weight, base):
        flat_weight = weight.reshape(-1, block)
        offset_ids = got_flat - base
        usable = jnp.logical_and(offset_ids >= 0, offset_ids < gate_blocks)
        row_index = jnp.where(usable, offset_ids, gate_blocks).astype(jnp.int32)
        fetched = jnp.take(flat_weight, jnp.minimum(row_index, gate_blocks - 1), axis=0).astype(
            jnp.float32
        )
        new_rows = (fetched + combined).astype(jnp.bfloat16)
        return flat_weight.at[row_index].set(new_rows, mode="drop").reshape(weight.shape)

    new_gate = updated(gate_weight, 0)
    new_up = updated(up_weight, gate_blocks)
    new_down = updated(down_weight, 2 * gate_blocks)
    token_rows, slice_width = tokens.shape
    picks = route_ids.reshape(-1)
    expert_hits = (picks[:, None] == jnp.arange(EXPERTS, dtype=jnp.int32)[None, :]).astype(
        jnp.int32
    )
    expert_before = jnp.cumsum(expert_hits, axis=0) - expert_hits
    slot = picks * CAP + jnp.sum(expert_before * expert_hits, axis=1)
    slot_match = (slot[None, :] == jnp.arange(EXPERTS * CAP, dtype=jnp.int32)[:, None]).reshape(
        EXPERTS * CAP, token_rows, TOP
    )
    full_rows = lax.all_gather(tokens, "tp", axis=1, tiled=True)
    outgoing = row_norm(full_rows, norm_gain, width)
    feature_count = outgoing.shape[1]
    slot_rows = jnp.any(slot_match, axis=2).astype(jnp.bfloat16)
    sending = jnp.dot(slot_rows, outgoing, preferred_element_type=jnp.float32).astype(jnp.bfloat16)
    sending = sending.reshape(ep_count, exp_dev, CAP, feature_count)
    normed = lax.all_to_all(sending, "ep", split_axis=0, concat_axis=0, tiled=True)
    gate = jnp.einsum("secd,efd->secf", normed, new_gate, preferred_element_type=jnp.float32)
    up = jnp.einsum("secd,efd->secf", normed, new_up, preferred_element_type=jnp.float32)
    gate, up = (gate, up)
    hidden = (jax.nn.silu(gate) * up).astype(jnp.bfloat16)
    partial_value = jnp.einsum(
        "secf,edf->secd", hidden, new_down, preferred_element_type=jnp.float32
    ).astype(jnp.bfloat16)
    results = lax.all_to_all(partial_value, "ep", split_axis=0, concat_axis=0, tiled=True)
    result_width = results.shape[3]
    flat_results = results.reshape(EXPERTS * CAP, result_width).astype(jnp.float32)
    shares = route_scores / jnp.sum(route_scores, axis=1, keepdims=True)
    slot_shares = jnp.sum(jnp.where(slot_match, shares[None, :, :], 0.0), axis=2)
    weighted = jnp.einsum("st,sd->td", slot_shares, flat_results, precision=lax.Precision.HIGHEST)
    return lax.psum_scatter(weighted.astype(jnp.bfloat16), "tp", scatter_dimension=1, tiled=True)


MAX_ROWS = 512
SUB = 1 << 15
NOTE_ROWS = 16
MESH = pl.DeviceIdType.MESH


def partners():
    z, c = lax.axis_index("ep"), lax.axis_index("tp")
    return z, c, lax.rem(c + 2, 4), c + 1 - 2 * lax.rem(c, 2)


def greet(z, far, near, ep_count):
    barrier = pltpu.get_barrier_semaphore()
    for k in range(1, ep_count):
        pl.semaphore_signal(
            barrier, inc=1, device_id={"ep": lax.rem(z + k, ep_count)}, device_id_type=MESH
        )
    for other in (far, near):
        pl.semaphore_signal(barrier, inc=1, device_id={"tp": other}, device_id_type=MESH)
    pl.semaphore_wait(barrier, ep_count + 1)


def send(source, target, send_sem, recv_sem, device):
    copy = pltpu.make_async_remote_copy(
        src_ref=source,
        dst_ref=target,
        send_sem=send_sem,
        recv_sem=recv_sem,
        device_id=device,
        device_id_type=MESH,
    )
    copy.start()
    return copy


def gather_kernel(tokens, codes, notes, all_tokens, all_codes, all_notes, sent, came, own_sem):
    ep_count = all_tokens.shape[1]
    z, c, far, near = partners()
    own = []
    for i, (mine, slot) in enumerate(
        ((tokens, all_tokens.at[c, z]), (codes, all_codes.at[z]), (notes, all_notes.at[z]))
    ):
        copy = pltpu.make_async_copy(mine, slot, own_sem.at[i])
        copy.start()
        own.append(copy)
    greet(z, far, near, ep_count)
    others = range(1, ep_count)
    used = iter(range(sent.shape[0]))

    def launch(source, target, device):
        at = next(used)
        return send(source, target, sent.at[at], came.at[at], device)

    def peer(k):
        return {"ep": lax.rem(z + k, ep_count)}

    told = [launch(notes, all_notes.at[z], peer(k)) for k in others]
    rows = [launch(tokens, all_tokens.at[c, z], peer(k)) for k in others]
    slot = all_tokens.at[c, z]
    across = [launch(tokens, slot, {"tp": far})]
    beside = [launch(tokens, slot, {"tp": near})]
    blocks = [launch(codes, all_codes.at[z], peer(k)) for k in others]
    for k in others:
        rows[k - 1].wait_recv()
        slot = all_tokens.at[c, lax.rem(z + ep_count - k, ep_count)]
        across.append(launch(slot, slot, {"tp": far}))
        beside.append(launch(slot, slot, {"tp": near}))
    for k in range(ep_count):
        across[k].wait_recv()
        slot = all_tokens.at[far, lax.rem(z + ep_count - k, ep_count)]
        beside.append(launch(slot, slot, {"tp": near}))
    for copy in told + blocks + beside:
        copy.wait_recv()
    for copy in told + blocks + beside + rows + across:
        copy.wait_send()
    for copy in own:
        copy.wait()


def gather(tokens, codes, notes, ep_count, tp_count):
    copies = 3 * (ep_count - 1) + 3 * ep_count
    vmem = pl.BlockSpec(memory_space=pltpu.VMEM)
    return pl.pallas_call(
        gather_kernel,
        out_shape=[
            jax.ShapeDtypeStruct((tp_count, ep_count) + tokens.shape, tokens.dtype),
            jax.ShapeDtypeStruct((ep_count,) + codes.shape, codes.dtype),
            jax.ShapeDtypeStruct((ep_count,) + notes.shape, notes.dtype),
        ],
        in_specs=[vmem] * 3,
        out_specs=[vmem] * 3,
        scratch_shapes=[
            pltpu.SemaphoreType.DMA((copies,)),
            pltpu.SemaphoreType.DMA((copies,)),
            pltpu.SemaphoreType.DMA((3,)),
        ],
        compiler_params=pltpu.CompilerParams(
            collective_id=0, has_side_effects=True, vmem_limit_bytes=16 << 20
        ),
    )(tokens, codes, notes)


def scatter_kernel(
    sums, out, first, second, third, to_far, to_peer, sent, came
):
    ep_count = sums.shape[1]
    z, c, far, near = partners()
    beyond = far + 1 - 2 * lax.rem(far, 2)
    greet(z, far, near, ep_count)
    used = iter(range(sent.shape[0]))

    def launch(source, target, device):
        at = next(used)
        return send(source, target, sent.at[at], came.at[at], device)

    order = [lax.rem(z + k, ep_count) for k in list(range(1, ep_count)) + [0]]
    relayed = [launch(sums.at[beyond, j], first.at[0, j], {"tp": near}) for j in order]
    direct = [launch(sums.at[near, j], first.at[1, j], {"tp": near}) for j in order]

    def wide(block):
        return block.astype(jnp.float32)

    across = []
    for copy, j in zip(relayed, order):
        copy.wait_recv()
        to_far[j] = (wide(sums[far, j]) + wide(first[0, j])).astype(jnp.bfloat16)
        across.append(launch(to_far.at[j], second.at[j], {"tp": far}))
    peers = []
    for k, j in enumerate(order):
        direct[k].wait_recv()
        across[k].wait_recv()
        summed = wide(sums[c, j]) + wide(first[1, j]) + wide(second[j])
        if k < ep_count - 1:
            to_peer[k] = summed.astype(jnp.bfloat16)
            peers.append(launch(to_peer.at[k], third.at[k], {"ep": j}))
    for k, copy in enumerate(peers):
        copy.wait_recv()
        summed = summed + wide(third[k])
    out[...] = summed.astype(jnp.bfloat16)
    for copy in relayed + direct + across + peers:
        copy.wait_send()


def scatter_sums(sums):
    tp_count, ep_count = sums.shape[:2]
    block = sums.shape[2:]
    copies = 4 * ep_count - 1
    vmem = pl.BlockSpec(memory_space=pltpu.VMEM)
    return pl.pallas_call(
        scatter_kernel,
        out_shape=jax.ShapeDtypeStruct(block, jnp.bfloat16),
        in_specs=[vmem],
        out_specs=vmem,
        scratch_shapes=[
            pltpu.VMEM((2, ep_count) + block, jnp.bfloat16),
            pltpu.VMEM((ep_count,) + block, jnp.bfloat16),
            pltpu.VMEM((ep_count - 1,) + block, jnp.bfloat16),
            pltpu.VMEM((ep_count,) + block, jnp.bfloat16),
            pltpu.VMEM((ep_count - 1,) + block, jnp.bfloat16),
            pltpu.SemaphoreType.DMA((copies,)),
            pltpu.SemaphoreType.DMA((copies,)),
        ],
        compiler_params=pltpu.CompilerParams(
            collective_id=1, has_side_effects=True, vmem_limit_bytes=16 << 20
        ),
    )(sums)


def expert_kernel(
    table, begins, rank, tokens, gain, ids, scores, values, gate, up, down, out, normed, total
):
    step = pl.program_id(0)
    exp_dev = pl.num_programs(0)
    tp_count, ep_count, rows, part = tokens.shape
    width = tp_count * part

    @pl.when(step == 0)
    def _():
        for i in range(ep_count):
            scale = jnp.zeros((rows, 1), jnp.float32)
            for c in range(tp_count):
                floats = tokens[c, i].astype(jnp.float32)
                scale += jnp.sum(floats * floats, axis=1, keepdims=True)
            scale = lax.rsqrt(scale / width + EPS)
            for c in range(tp_count):
                span = slice(c * part, (c + 1) * part)
                total[span, i * rows : (i + 1) * rows] = (
                    tokens[c, i].astype(jnp.float32) * scale * gain[:, span]
                ).T
        normed[...] = total[...].astype(jnp.bfloat16)
        total[...] = jnp.zeros_like(total)

    line = lax.broadcasted_iota(jnp.int32, (16, 128), 0)
    starts = [begins[3 * step + m] for m in range(3)]
    counts = [begins[3 * step + m + 1] - starts[m] for m in range(3)]

    @pl.loop(0, jnp.maximum(jnp.maximum(counts[0], counts[1]), counts[2]))
    def _(n):
        for m, weight in enumerate((gate, up, down)):
            valid = n < counts[m]
            b = jnp.where(valid, starts[m] + n, 0)
            place = jnp.where(valid, table[b], 0)
            row, column = place // 16, place % 16
            first = pl.multiple_of(row // 16 * 16, 16)
            where = (0, pl.ds(first, 16), pl.ds(pl.multiple_of(column * 128, 128), 128))
            at = jnp.where(valid, row - first, -1)
            added = jnp.where(line == at, values[pl.ds(b, 1), :], 0.0)
            weight[where] = (weight[where].astype(jnp.float32) + added).astype(jnp.bfloat16)

    picked = jnp.where(ids[...] == rank[0] * exp_dev + step, scores[...], 0.0)
    share = jnp.sum(picked, axis=0, keepdims=True) / jnp.sum(scores[...], axis=0, keepdims=True)
    gated = jnp.dot(gate[0], normed[...], preferred_element_type=jnp.float32)
    upped = jnp.dot(up[0], normed[...], preferred_element_type=jnp.float32)
    hidden = (gated / (1.0 + jnp.exp(-gated)) * upped * share).astype(jnp.bfloat16)
    for c in range(tp_count):
        span = slice(c * part, (c + 1) * part)
        total[span, :] += jnp.dot(down[0, span, :], hidden, preferred_element_type=jnp.float32)

    @pl.when(step == exp_dev - 1)
    def _():
        for c in range(tp_count):
            turned = total[c * part : (c + 1) * part, :].T
            for i in range(ep_count):
                out[c, i] = turned[i * rows : (i + 1) * rows, :].astype(jnp.bfloat16)


def expert_sums(table, begins, rank, tokens, gain, ids, scores, values, gate, up, down):
    tp_count, ep_count, rows, part = tokens.shape
    exp_dev, ff_local, width = gate.shape

    def held(array):
        return pl.BlockSpec(array.shape, lambda step, *_: (0,) * array.ndim)

    def one(array):
        return pl.BlockSpec((1,) + array.shape[1:], lambda step, *_: (step, 0, 0))

    return pl.pallas_call(
        expert_kernel,
        out_shape=jax.ShapeDtypeStruct(tokens.shape, jnp.bfloat16),
        grid_spec=pltpu.PrefetchScalarGridSpec(
            num_scalar_prefetch=3,
            grid=(exp_dev,),
            in_specs=[held(tokens), held(gain), held(ids.T), held(scores.T), held(values)]
            + [one(gate), one(up), one(down)],
            out_specs=held(tokens),
            scratch_shapes=[
                pltpu.VMEM((width, ep_count * rows), jnp.bfloat16),
                pltpu.VMEM((width, ep_count * rows), jnp.float32),
            ],
        ),
        compiler_params=pltpu.CompilerParams(vmem_limit_bytes=40 << 20),
    )(table, begins, rank, tokens, gain, ids.T, scores.T, values, gate, up, down)


def sorted_updates(owned, placing, values, ep_count, exp_dev, ff_local, width, limit):
    block = values.shape[1]
    count = values.shape[0]
    learner = jnp.arange(count, dtype=jnp.int32) // (count // ep_count)
    per_row, per_down = width // block, ff_local // block
    ff_rows, d_rows = ff_local // ep_count, width // ep_count
    span = ff_rows * per_row
    places = 2 * span + d_rows * per_down
    spot = placing % places
    matrix = jnp.minimum(spot // span, 2)
    remain = spot - matrix * span
    row_up, column_up = learner * ff_rows + remain // per_row, remain % per_row
    row_down, column_down = learner * d_rows + remain // per_down, remain % per_down
    row = jnp.where(matrix == 2, row_down, row_up)
    column = jnp.where(matrix == 2, column_down, column_up)
    target = (placing // places * 3 + matrix) * SUB + row * 16 + column
    target = jnp.where(owned, target, 1 << 30)
    order = jnp.arange(count, dtype=jnp.int32)
    ahead = jnp.logical_or(
        target[None, :] < target[:, None],
        jnp.logical_and(target[None, :] == target[:, None], order[None, :] < order[:, None]),
    )
    position = jnp.sum(ahead.astype(jnp.int32), axis=1)
    chosen = position[None, :] == jnp.arange(limit, dtype=jnp.int32)[:, None]
    ordered = jnp.sum(jnp.where(chosen, target[None, :], 0), axis=1)
    same = (ordered[:, None] == target[None, :]).astype(jnp.bfloat16)
    combined = jnp.dot(same, values, preferred_element_type=jnp.float32)
    repeated = jnp.concatenate([jnp.zeros((1,), jnp.bool_), ordered[1:] == ordered[:-1]])
    combined = jnp.where(repeated[:, None], 0.0, combined)
    edges = jnp.arange(3 * exp_dev + 1, dtype=jnp.int32) * SUB
    begins = jnp.sum((target[None, :] < edges[:, None]).astype(jnp.int32), axis=1)
    return ordered % SUB, begins, combined


def gathered(
    tokens,
    norm_gain,
    route_ids,
    route_scores,
    gate_weight,
    up_weight,
    down_weight,
    delta_codes,
    delta_exps,
    delta_owner,
    delta_places,
):
    ep_count, tp_count = lax.axis_size("ep"), lax.axis_size("tp")
    ep_rank = lax.axis_index("ep")
    exp_dev, ff_local, width = gate_weight.shape
    block_count, block = delta_codes.shape[2:]
    rows = tokens.shape[0]
    limit = block_count * 5 // (2 * ep_count) * ep_count

    numbers = [delta_exps, delta_owner, delta_places, route_ids, route_scores]
    notes = jnp.concatenate([number.astype(jnp.float32).reshape(-1) for number in numbers])
    notes = jnp.pad(notes, (0, NOTE_ROWS * block - notes.shape[0])).reshape(NOTE_ROWS, block)
    got_tokens, got_codes, got_notes = gather(
        tokens, delta_codes[0, 0], notes, ep_count, tp_count
    )
    got_notes = got_notes.reshape(ep_count, -1)
    picks = rows * TOP
    cuts = [0, block_count, 2 * block_count, 3 * block_count]
    cuts += [cuts[3] + picks, cuts[3] + 2 * picks]
    exps, owner, placing, ids, scores = (
        got_notes[:, cuts[k] : cuts[k + 1]].reshape(-1) for k in range(5)
    )
    owner, placing = owner.astype(jnp.int32), placing.astype(jnp.int32)
    ids = ids.astype(jnp.int32).reshape(-1, TOP)
    scores = scores.reshape(-1, TOP)
    got_values = got_codes.reshape(-1, block).astype(jnp.float32) * jnp.exp2(exps)[:, None]
    got_values = got_values.astype(jnp.bfloat16)
    table, begins, values = sorted_updates(
        owner == ep_rank, placing, got_values, ep_count, exp_dev, ff_local, width, limit
    )
    sums = expert_sums(
        table,
        begins,
        ep_rank.reshape(1).astype(jnp.int32),
        got_tokens,
        norm_gain.reshape(1, -1),
        ids,
        scores,
        values,
        gate_weight,
        up_weight,
        down_weight,
    )
    return scatter_sums(sums)


def per_device(*args):
    few = args[0].shape[0] * lax.axis_size("ep") <= MAX_ROWS and lax.axis_size("tp") == 4
    return gathered(*args) if few else routed(*args)


def solution(mesh):
    placed = (
        P(("groups", "ep"), "tp"),
        P(),
        P(("groups", "ep"), None),
        P(("groups", "ep"), None),
        P(("groups", "ep"), "tp", None),
        P(("groups", "ep"), "tp", None),
        P(("groups", "ep"), None, "tp"),
        P(("groups", "ep"), "tp", None, None),
        P(("groups", "ep"), "tp", None),
        P(("groups", "ep"), "tp", None, None),
        P(("groups", "ep"), "tp", None),
    )
    return jax.shard_map(
        per_device, mesh=mesh, in_specs=placed, out_specs=P(("groups", "ep"), "tp"), check_vma=False
    )
```
